32 devices in a mesh: expert: 8 (over z, x), slab: 4 (over y, core).
Axes of the slice: x: 2, y: 2, z: 4, core: 2. Of those that a mesh axis runs over, the one named last changes fastest.
Arguments:
- tokens: bfloat16 [8192, 768], P('expert', 'slab'), may hold values from -6 to 6
- gate: float32 [8192], P('expert'), may hold values from 0.2 to 1
- routes: int32 [8192, 1], P('expert'), may hold values from 0 to 31; in each aligned block of 1024 rows (0 to 1023, 1024 to 2047, ...) at most 64 rows name the same one
- grad_out: bfloat16 [8192, 768], P('expert', 'slab'), may hold values from -6 to 6
- w_in: bfloat16 [32, 768, 3072], P('expert', None, 'slab'), may hold values from -0.21875 to 0.21875
- w_out: bfloat16 [32, 3072, 768], P('expert', 'slab'), may hold values from -0.109375 to 0.109375
Outputs:
- mixed: bfloat16 [8192, 768], P('expert', 'slab')
- grad_in: bfloat16 [8192, 768], P('expert', 'slab')
- grad_w_in: bfloat16 [32, 768, 3072], P('expert', None, 'slab')
- grad_w_out: bfloat16 [32, 3072, 768], P('expert', 'slab')
The draws below stay inside these ranges and needn't reach their ends.
Inputs may be any that keep to these rules, and one draw needn't show every extreme that they name: `routes`: in each aligned block of 1024 rows no expert is named by more than 64 rows, a bound that some block reaches.
All inputs are finite; a program needn't handle non-finite values.
Results may differ from the reference program's by a relative error of at most 0.0095.
Values may be sent and summed in bfloat16 or wider, within the bound.
A program may use at most 128 MiB of HBM per device.

```python
import math
import jax
import jax.numpy as jnp
import numpy as np
from jax import lax

D = 768
FF = 3072
TOK_DEV = 1024
EXPERTS = 32
CAP = 64
TOKENS = 8192
N_EXPERT = 8
N_SLAB = 4


def shard_levels(stream_key, extent, shards, least, high):
    factor_of = 1.0
    for axis_at, blocks in shards:
        draws = jax.random.uniform(jax.random.fold_in(jax.random.fold_in(stream_key, 6), axis_at), (blocks,), jnp.float32, least / len(shards), high / len(shards))
        factor_of = factor_of * jnp.repeat(jnp.exp(draws), extent[axis_at] // blocks).reshape((-1,) + (1,) * (len(extent) - 1 - axis_at))
    return factor_of


def shared_out(own_key, own, number, rows, amount, top, reach, slope):
    ranking = jax.random.permutation(own_key, amount)
    crowded, usual = load_shares(amount, rows * top, reach, slope, True), load_shares(amount, rows * top, reach, slope, False)
    places = jnp.arange(amount)

    def named(sizes, offset_by):
        used = int((sizes > 0).sum())
        fixed = max(1, used // 4)
        moved = fixed + (places - fixed + offset_by * (used - fixed)) % max(1, amount - fixed)
        return jnp.zeros((amount,), jnp.int32).at[ranking[jnp.where(places < fixed, places, moved)]].set(jnp.asarray(sizes, jnp.int32))

    sizes = jnp.where(number % 4 == 0, named(crowded, number // 4), named(usual, number - number // 4 - 1))
    mixed = jax.random.permutation(jax.random.fold_in(own, 3), amount)
    donor, sink = mixed[0:amount // 2 * 2:2], mixed[1:amount // 2 * 2:2]
    margin = jnp.minimum(sizes[donor] - 1, reach - sizes[sink]) // 2
    margin = jnp.where((donor == ranking[0]) | (sink == ranking[0]) | (sizes[sink] == 0), 0, jnp.maximum(margin, 0))
    moved = jax.random.randint(jax.random.fold_in(own, 4), (amount // 2,), 0, 1 << 20) % (margin + 1)
    sizes = sizes.at[donor].add(-moved).at[sink].add(moved)
    members = jnp.searchsorted(jnp.cumsum(sizes), jnp.arange(rows * top), side="right").astype(jnp.int32)
    grid = members.reshape(top, rows).T
    grid = grid[jax.random.permutation(jax.random.fold_in(own, 1), rows)]
    offset_by = jax.random.randint(jax.random.fold_in(own, 2), (rows, 1), 0, top)
    return jnp.take_along_axis(grid, (jnp.arange(top)[None, :] + offset_by) % top, axis=1)


def load_shares(amount, total, most, slope, full):
    weights = [(1 << 20) // math.isqrt(standing ** slope) + 1 for standing in range(1, amount + 1)]
    largest = most if full else min(most, max(-(-total // amount), total * weights[0] // sum(weights)))
    least = 1 if total - largest >= amount - 1 else 0
    counts, rest = [largest] + [least] * (amount - 1), total - largest - least * (amount - 1)
    while rest > 0:
        free = [i for i in range(1, amount) if counts[i] < largest] or [i for i in range(1, amount) if counts[i] < most]
        whole, left = sum([weights[i] for i in free]), rest
        for i in free:
            addition = min(most - counts[i], max(1, left * weights[i] // whole), rest)
            counts[i] = counts[i] + addition
            rest = rest - addition
    return np.array(counts)


def centred(stream_key, dims, scale, most, shards=(), kind=jnp.bfloat16):
    array = jax.random.normal(stream_key, dims, jnp.float32) * scale
    if len(shards) > 0:
        array = shard_levels(stream_key, dims, shards, -0.22, 0.18) * array
    return jnp.clip(array, min=-most, max=most).astype(kind)


def setup_inputs(seed: int = 0) -> dict:
    key_list = jax.random.split(jax.random.key(seed), 7)
    tokens = centred(key_list[0], (TOKENS, D), 1.0, 6.0, ((0, 8), (1, 4)))
    gate = jnp.clip(0.2 + 0.8 * jax.random.uniform(key_list[1], (TOKENS,), jnp.float32) ** shard_levels(key_list[1], (TOKENS,), ((0, 8),), -0.2, 0.2), 0.2, 1.0)
    routes_keys = jax.random.split(jax.random.fold_in(key_list[2], 1), TOKENS // TOK_DEV)
    routes_turns = jax.random.permutation(jax.random.fold_in(key_list[2], 3), TOKENS // TOK_DEV)
    routes = jax.vmap(lambda own, number: shared_out(jax.random.fold_in(key_list[2], 2), own, number, TOK_DEV, EXPERTS, 1, CAP, 2))(routes_keys, routes_turns).reshape((TOKENS, 1))
    grad_out = centred(key_list[3], (TOKENS, D), 1.0, 6.0, ((0, 8), (1, 4)))
    w_in = centred(key_list[4], (EXPERTS, D, FF), D ** -0.5, 0.21875, ((0, 8), (2, 4)))
    w_out = centred(key_list[5], (EXPERTS, FF, D), FF ** -0.5, 0.109375, ((0, 8), (1, 4)))
    return {"tokens": tokens, "gate": gate, "routes": routes, "grad_out": grad_out, "w_in": w_in, "w_out": w_out}


def place_rows(routes):
    expert_ids = routes[:, 0].astype(jnp.int32)
    onehot = (expert_ids[:, None] == jnp.arange(EXPERTS, dtype=jnp.int32)[None, :]).astype(jnp.int32)
    blocks = onehot.reshape(N_EXPERT, TOK_DEV, EXPERTS)
    earlier = jnp.cumsum(blocks, axis=1) - blocks
    slot = jnp.sum(earlier * blocks, axis=2).reshape(-1).astype(jnp.int32)
    block_ids = (jnp.arange(TOKENS, dtype=jnp.int32) // TOK_DEV).astype(jnp.int32)
    return expert_ids, (block_ids * CAP + slot).astype(jnp.int32)


def slab_sum(left, right):
    width = FF // N_SLAB
    total = jnp.zeros((left.shape[0], right.shape[1]), jnp.float32)
    for index in range(N_SLAB):
        piece = jnp.dot(left[:, index * width:(index + 1) * width], right[index * width:(index + 1) * width, :], preferred_element_type=jnp.float32).astype(jnp.bfloat16)
        total = total + piece.astype(jnp.float32)
    return total.astype(jnp.bfloat16)


def expert_work(operands):
    rows, grads, weight_in, weight_out = operands
    pre = jnp.dot(rows, weight_in, preferred_element_type=jnp.float32)
    hidden = jnp.maximum(pre, 0.0).astype(jnp.bfloat16)
    out_rows = slab_sum(hidden, weight_out)
    grad_pre = jnp.dot(grads, weight_out.T, preferred_element_type=jnp.float32)
    grad_hidden = jnp.where(pre > 0.0, grad_pre, 0.0).astype(jnp.bfloat16)
    grad_wo = jnp.dot(hidden.T, grads, preferred_element_type=jnp.float32).astype(jnp.bfloat16)
    grad_wi = jnp.dot(rows.T, grad_hidden, preferred_element_type=jnp.float32).astype(jnp.bfloat16)
    grad_rows = slab_sum(grad_hidden, weight_in.T)
    return out_rows, grad_rows, grad_wi, grad_wo


def reference(tokens, gate, routes, grad_out, w_in, w_out):
    expert_ids, row_ids = place_rows(routes)
    scaled = (gate[:, None] * grad_out.astype(jnp.float32)).astype(jnp.bfloat16)
    empty = jnp.zeros((EXPERTS, N_EXPERT * CAP, D), jnp.bfloat16)
    rows_all = empty.at[expert_ids, row_ids].set(tokens)
    grads_all = empty.at[expert_ids, row_ids].set(scaled)
    out_rows, grad_rows, grad_w_in, grad_w_out = lax.map(expert_work, (rows_all, grads_all, w_in, w_out))
    picked = out_rows[expert_ids, row_ids].astype(jnp.float32)
    mixed = (gate[:, None] * picked).astype(jnp.bfloat16)
    grad_in = grad_rows[expert_ids, row_ids]
    return mixed, grad_in, grad_w_in, grad_w_out
```

```python
import functools

import jax
import jax.numpy as jnp
from jax import lax
from jax.experimental import pallas as pl
from jax.experimental.pallas import tpu as pltpu
from jax.sharding import PartitionSpec as P

MESH = pl.DeviceIdType.MESH
BF = jnp.bfloat16
F32 = jnp.float32


def flip(index, mask, count):
    out = index
    bit = 1
    while bit < count:
        if mask & bit:
            out = out + (1 - 2 * ((index // bit) % 2)) * bit
        bit *= 2
    return out


def dot(a, b, ca=1, cb=0):
    return lax.dot_general(a, b, (((ca,), (cb,)), ((), ())), preferred_element_type=F32)


def kernel(E, cap, L, TILE,
           trow, tcol, tok, grd, wi_h, wo_h,
           mix_o, gin_o, gwi_o, gwo_o,
           sib_t, sib_g, send_t, send_g, xb, gb, wi, wo, gwi, gwo, hid, gh,
           part, gpart, cb, gcb, ys, gys, yr, gyr, fin, gfin, back, gback,
           tp, gtp, rtp, rgtp, ssem, rsem, lsem):
    Lh = L // 2
    R = Lh * cap
    F = tok.shape[1]
    D = 2 * F
    rows = E * cap
    FS = wi.shape[2]
    T = tok.shape[0]
    e = lax.axis_index("expert")
    s = lax.axis_index("slab")
    h = s // 2
    c = s % 2
    sib = (e, 2 * h + 1 - c)
    ym = (e, 2 * (1 - h) + c)

    load_wi = pltpu.make_async_copy(wi_h, wi, lsem.at[0])
    load_wo = pltpu.make_async_copy(wo_h, wo, lsem.at[1])
    load_wi.start()
    load_wo.start()

    barrier = pltpu.get_barrier_semaphore()
    peers = [sib, ym] + [(flip(e, k, E), s) for k in range(1, E)]
    for p in peers:
        pl.semaphore_signal(barrier, inc=1, device_id=p, device_id_type=MESH)
    pl.semaphore_wait(barrier, len(peers))

    started = []

    def send(src, dst, dev):
        n = len(started)
        copy = pltpu.make_async_remote_copy(
            src_ref=src, dst_ref=dst, send_sem=ssem.at[n], recv_sem=rsem.at[n],
            device_id=dev, device_id_type=MESH)
        copy.start()
        started.append(copy)
        return copy

    order = list(range(E - 1, 0, -1))
    mine = pl.ds(c * Lh, Lh)

    c_t = send(tok, sib_t, sib)
    c_g = send(grd, sib_g, sib)

    def scatter(copy, own, other, stage, buf):
        copy.wait_recv()
        other[...] = own[...] + other[...]
        a2a = {}
        for k in order + [0]:
            dest = flip(e, k, E)
            row = lax.broadcasted_iota(jnp.int32, (R, T), 0) + dest * R
            place = jnp.where(row == trow[...], 1.0, 0.0).astype(BF)
            val = dot(place, other[...]).astype(BF).reshape(Lh, cap, F)
            if k == 0:
                buf[h, mine, e] = val
            else:
                stage[k] = val
                a2a[k] = send(stage.at[k], buf.at[h, mine, e], (dest, s))
        return a2a

    ycopy = {}
    waits = {"t": [], "g": []}

    def pass_on(tag, buf, a2a, k):
        if k:
            a2a[k].wait_recv()
        ref = buf.at[h, mine, flip(e, k, E)]
        ycopy[tag, k] = send(ref, ref, ym)
        waits[tag].append(send(ref, ref, sib))

    def pass_y(tag, buf, k):
        ycopy[tag, k].wait_recv()
        ref = buf.at[1 - h, mine, flip(e, k, E)]
        waits[tag].append(send(ref, ref, sib))

    a2a_t = scatter(c_t, tok, sib_t, send_t, xb)
    pass_on("t", xb, a2a_t, 0)
    a2a_g = scatter(c_g, grd, sib_g, send_g, gb)
    arrive = [0] + order[::-1]
    for i, k in enumerate(arrive):
        if k:
            pass_on("t", xb, a2a_t, k)
        if i >= 2:
            pass_y("t", xb, arrive[i - 2])
    for k in arrive[-2:]:
        pass_y("t", xb, k)
    for w in waits["t"]:
        w.wait_recv()
    load_wi.wait()
    load_wo.wait()

    def whole(buf, l):
        return jnp.concatenate(
            [buf[0, l].reshape(rows, F), buf[1, l].reshape(rows, F)], axis=1)

    def tile(n):
        return pl.ds(pl.multiple_of(n * TILE, TILE), TILE)

    def forward(l):
        @pl.loop(0, FS // TILE)
        def _(n):
            pre = dot(whole(xb, l), wi[l, :, tile(n)])
            hid[l, :, tile(n)] = jnp.maximum(pre, 0.0).astype(BF)

        @pl.loop(0, D // TILE)
        def _(n):
            part[l, :, tile(n)] = dot(hid[l], wo[l, :, tile(n)]).astype(BF)

    def backward(l):
        @pl.loop(0, FS // TILE)
        def _(n):
            g = dot(whole(gb, l), wo[l, tile(n), :], 1, 1)
            gh[l, :, tile(n)] = jnp.where(
                hid[l, :, tile(n)].astype(F32) > 0.0, g, 0.0).astype(BF)

        @pl.loop(0, D // TILE)
        def _(n):
            gpart[l, :, tile(n)] = dot(gh[l], wi[l, tile(n), :], 1, 1).astype(BF)

    stores = []

    def weights(l):
        @pl.loop(0, FS // TILE)
        def _(n):
            gwo[l, tile(n), :] = dot(hid[l, :, tile(n)], whole(gb, l), 0, 0).astype(BF)

        put = pltpu.make_async_copy(gwo.at[l], gwo_o.at[l], lsem.at[2 + 2 * l])
        put.start()
        stores.append(put)

        @pl.loop(0, 2)
        def _(n):
            gwi[l, pl.ds(pl.multiple_of(n * F, F), F), :] = dot(
                xb[n, l].reshape(rows, F), gh[l], 0, 0).astype(BF)

        put = pltpu.make_async_copy(gwi.at[l], gwi_o.at[l], lsem.at[3 + 2 * l])
        put.start()
        stores.append(put)

    def half(which):
        return pl.ds(pl.multiple_of(which * F, 128), F)

    def combine(copy, own, other, stage, land, j):
        copy.wait_recv()
        l = c * Lh + j
        stage[j] = (own[l, :, half(1 - h)].astype(F32)
                    + other[j, :, half(1 - h)].astype(F32)).astype(BF)
        return send(stage.at[j], land.at[j], ym)

    def finish(copy, own, other, land, final, out, j):
        copy.wait_recv()
        l = c * Lh + j
        total = (own[l, :, half(h)].astype(F32) + other[j, :, half(h)].astype(F32)
                 + land[j].astype(F32)).astype(BF)
        final[j] = total.reshape(E, cap, F)
        res = []
        for k in order:
            dest = flip(e, k, E)
            res.append(send(final.at[j, dest], out.at[e, j], (dest, s)))
        out[e, j] = final[j, e]
        return res

    share = -(-E // L)
    csend = []
    for j in range(Lh):
        l = (1 - c) * Lh + j
        forward(l)
        csend.append(send(part.at[l], cb.at[j], sib))
        for k in arrive[j * share:(j + 1) * share]:
            pass_on("g", gb, a2a_g, k)
    for j in range(Lh, L):
        forward(c * Lh + j - Lh)
        for k in arrive[j * share:(j + 1) * share]:
            pass_on("g", gb, a2a_g, k)
    ysend = [combine(csend[j], part, cb, ys, yr, j) for j in range(Lh)]
    for k in arrive:
        pass_y("g", gb, k)
    for w in waits["g"]:
        w.wait_recv()

    gcsend, bsend, gbsend = [], [], []
    for j in range(Lh):
        l = (1 - c) * Lh + j
        backward(l)
        gcsend.append(send(gpart.at[l], gcb.at[j], sib))
    gysend = []
    for j in range(Lh):
        backward(c * Lh + j)
        gysend.append(combine(gcsend[j], gpart, gcb, gys, gyr, j))
        bsend += finish(ysend[j], part, cb, yr, fin, back, j)
    for l in range(L):
        weights(l)
        if l % 2:
            gbsend += finish(gysend[l // 2], gpart, gcb, gyr, gfin, gback, l // 2)

    def collect(copies, out, stage, land):
        for w in copies:
            w.wait_recv()

        @pl.loop(0, T // 256)
        def _(n):
            at = pl.ds(pl.multiple_of(n * 256, 256), 256)
            row = lax.broadcasted_iota(jnp.int32, (256, E * R), 1)
            pick = jnp.where(row == tcol[at, :], 1.0, 0.0).astype(BF)
            stage[at, :] = dot(pick, out[...].reshape(E * R, F)).astype(BF)

        return send(stage, land, sib)

    last = collect(bsend, back, tp, rtp)
    glast = collect(gbsend, gback, gtp, rgtp)
    last.wait_recv()
    mix_o[...] = tp[...] + rtp[...]
    glast.wait_recv()
    gin_o[...] = gtp[...] + rgtp[...]
    for copy in started:
        copy.wait_send()
    for put in stores:
        put.wait()


def shards(tokens, gate, routes, grad_out, w_in, w_out):
    T, Q = tokens.shape
    E = lax.axis_size("expert")
    L, D, FS = w_in.shape
    X = E * L
    cap = 2 * T // X
    Lh = L // 2
    F = 2 * Q
    c = lax.axis_index("slab") % 2
    ids = routes[:, 0]
    onehot = ids[:, None] == jnp.arange(X, dtype=jnp.int32)[None, :]
    at = jnp.arange(T, dtype=jnp.int32)
    before = (at[:, None] > at[None, :]).astype(BF)
    earlier = jnp.dot(before, onehot.astype(BF), preferred_element_type=F32)
    slot = jnp.sum(jnp.where(onehot, earlier, 0.0), axis=1).astype(jnp.int32)
    local = ids % L
    target = jnp.where(
        local // Lh == c, (ids // L) * (Lh * cap) + (local % Lh) * cap + slot, -1)
    scaled = (gate[:, None] * grad_out.astype(F32)).astype(BF)

    def widen(v):
        z = jnp.zeros_like(v)
        return jnp.where(c == 0, jnp.concatenate([v, z], 1), jnp.concatenate([z, v], 1))

    rows = E * cap
    TILE = 256
    n_sem = 2 * (6 * E + 3)
    vm = lambda shape, t=BF: pltpu.VMEM(shape, t)
    two = lambda shape: [vm(shape), vm(shape)]
    scratch = (
        two((T, F)) + two((E, Lh, cap, F)) + two((2, L, E, cap, F))
        + two((L, D, FS)) + [vm((L, D, FS)), vm((L, FS, D))]
        + two((L, rows, FS)) + two((L, rows, D)) + two((Lh, rows, D))
        + two((Lh, rows, F)) + two((Lh, rows, F)) + two((Lh, E, cap, F))
        + two((E, Lh, cap, F)) + two((T, F)) + two((T, F))
        + [pltpu.SemaphoreType.DMA((n_sem,)), pltpu.SemaphoreType.DMA((n_sem,)),
           pltpu.SemaphoreType.DMA((2 + 2 * L,))])
    V = pl.BlockSpec(memory_space=pltpu.VMEM)
    A = pl.BlockSpec(memory_space=pl.ANY)
    mix, gin, gwi, gwo = pl.pallas_call(
        functools.partial(kernel, E, cap, L, TILE),
        out_shape=(
            jax.ShapeDtypeStruct((T, F), BF), jax.ShapeDtypeStruct((T, F), BF),
            jax.ShapeDtypeStruct(w_in.shape, BF), jax.ShapeDtypeStruct(w_out.shape, BF)),
        in_specs=[V, V, V, V, A, A],
        out_specs=(V, V, A, A),
        scratch_shapes=scratch,
        compiler_params=pltpu.CompilerParams(
            collective_id=0, has_side_effects=True, vmem_limit_bytes=63 * 2**20),
        cost_estimate=pl.CostEstimate(
            flops=12 * L * rows * D * FS, bytes_accessed=8 * L * D * FS, transcendentals=0),
    )(target[None, :], target[:, None], widen(tokens), widen(scaled), w_in, w_out)
    mix = lax.dynamic_slice(mix, (0, c * Q), (T, Q))
    gin = lax.dynamic_slice(gin, (0, c * Q), (T, Q))
    mixed = (gate[:, None] * mix.astype(F32)).astype(BF)
    return (mixed, gin, gwi, gwo)


def solution(mesh):
    in_specs = (
        P("expert", "slab"),
        P("expert"),
        P("expert", None),
        P("expert", "slab"),
        P("expert", None, "slab"),
        P("expert", "slab", None),
    )
    out_specs = (
        P("expert", "slab"),
        P("expert", "slab"),
        P("expert", None, "slab"),
        P("expert", "slab", None),
    )
    return jax.shard_map(shards, mesh=mesh, in_specs=in_specs, out_specs=out_specs, check_vma=False)
```

```python
import functools

import jax
import jax.numpy as jnp
from jax import lax
from jax.experimental import pallas as pl
from jax.experimental.pallas import tpu as pltpu
from jax.sharding import PartitionSpec as P

MESH = pl.DeviceIdType.MESH
BF = jnp.bfloat16
F32 = jnp.float32


def flip(index, mask, count):
    out = index
    bit = 1
    while bit < count:
        if mask & bit:
            out = out + (1 - 2 * ((index // bit) % 2)) * bit
        bit *= 2
    return out


def dot(a, b, ca=1, cb=0):
    return lax.dot_general(a, b, (((ca,), (cb,)), ((), ())), preferred_element_type=F32)


def kernel(E, cap, L, TILE,
           routes, gate, tok, grd, wi_h, wo_h,
           mix_o, gin_o, gwi_o, gwo_o,
           trow, cat_t, cat_g, send_t, send_g, xb, gb, wi, wo, gwi, gwo, hid, gh,
           part, gpart, cb, gcb, ys, gys, yr, gyr, fin, gfin, back, gback,
           tp, gtp, rtp, rgtp, ssem, rsem, lsem):
    Lh = L // 2
    R = Lh * cap
    Q, T = tok.shape
    F = 2 * Q
    D = 2 * F
    X = E * L
    rows = E * cap
    FS = wi.shape[2]
    e = lax.axis_index("expert")
    s = lax.axis_index("slab")
    h = s // 2
    c = s % 2
    sib = (e, 2 * h + 1 - c)
    ym = (e, 2 * (1 - h) + c)

    load_wi = pltpu.make_async_copy(wi_h, wi, lsem.at[0])
    load_wo = pltpu.make_async_copy(wo_h, wo, lsem.at[1])
    load_wi.start()
    load_wo.start()

    barrier = pltpu.get_barrier_semaphore()
    peers = [sib, ym] + [(flip(e, k, E), s) for k in range(1, E)]
    for p in peers:
        pl.semaphore_signal(barrier, inc=1, device_id=p, device_id_type=MESH)

    ids = routes[...]
    onehot = (lax.broadcasted_iota(jnp.int32, (X, T), 0) == ids).astype(F32)
    STEP = 256
    for n in range(T // STEP):
        at = slice(n * STEP, (n + 1) * STEP)
        before = (lax.broadcasted_iota(jnp.int32, (T, STEP), 0)
                  < lax.broadcasted_iota(jnp.int32, (T, STEP), 1) + n * STEP)
        earlier = dot(onehot.astype(BF), jnp.where(before, 1.0, 0.0).astype(BF))
        slot = jnp.sum(earlier * onehot[:, at], axis=0, keepdims=True).astype(jnp.int32)
        local = lax.rem(ids[:, at], L)
        trow[:, at] = jnp.where(
            lax.div(local, Lh) == c,
            lax.div(ids[:, at], L) * R + lax.rem(local, Lh) * cap + slot, -1)
    cat_g[c] = (gate[...] * grd[...].astype(F32)).astype(BF)
    cat_t[c] = tok[...]
    pl.semaphore_wait(barrier, len(peers))

    started = []

    def send(src, dst, dev):
        n = len(started)
        copy = pltpu.make_async_remote_copy(
            src_ref=src, dst_ref=dst, send_sem=ssem.at[n], recv_sem=rsem.at[n],
            device_id=dev, device_id_type=MESH)
        copy.start()
        started.append(copy)
        return copy

    far, near = list(range(E // 2, E)), list(range(1, E // 2))
    order = [k for i, f in enumerate(far) for k in ([f] + near[i:i + 1])]
    mine = pl.ds(c * Lh, Lh)

    c_t = send(cat_t.at[c], cat_t.at[c], sib)
    c_g = send(cat_g.at[c], cat_g.at[c], sib)

    def scatter(k, cat, stage, buf):
        dest = flip(e, k, E)
        row = lax.broadcasted_iota(jnp.int32, (R, T), 0) + dest * R
        place = jnp.where(row == trow[...], 1.0, 0.0).astype(BF)
        val = dot(place, cat[...].reshape(F, T), 1, 1).astype(BF).reshape(Lh, cap, F)
        if k == 0:
            buf[h, mine, e] = val
            return None
        stage[k] = val
        return send(stage.at[k], buf.at[h, mine, e], (dest, s))

    ycopy = {}
    waits = {"t": [], "g": []}

    def pass_on(tag, buf, a2a, k):
        if k:
            a2a[k].wait_recv()
        ref = buf.at[h, mine, flip(e, k, E)]
        ycopy[tag, k] = send(ref, ref, ym)
        waits[tag].append(send(ref, ref, sib))

    def pass_y(tag, buf, k):
        ycopy[tag, k].wait_recv()
        ref = buf.at[1 - h, mine, flip(e, k, E)]
        waits[tag].append(send(ref, ref, sib))

    arrive = [0] + order
    c_t.wait_recv()
    a2a_t = {k: scatter(k, cat_t, send_t, xb) for k in order + [0]}
    c_g.wait_recv()
    a2a_g = {}
    for i, k in enumerate(arrive):
        pass_on("t", xb, a2a_t, k)
        g = arrive[(i + 1) % E]
        a2a_g[g] = scatter(g, cat_g, send_g, gb)
        if i >= 2:
            pass_y("t", xb, arrive[i - 2])
    for k in arrive[-2:]:
        pass_y("t", xb, k)
    for w in waits["t"]:
        w.wait_recv()
    load_wi.wait()
    load_wo.wait()

    def whole(buf, l):
        return jnp.concatenate(
            [buf[0, l].reshape(rows, F), buf[1, l].reshape(rows, F)], axis=1)

    def tile(n):
        return pl.ds(pl.multiple_of(n * TILE, TILE), TILE)

    def forward(l):
        @pl.loop(0, FS // TILE)
        def _(n):
            pre = dot(whole(xb, l), wi[l, :, tile(n)])
            hid[l, :, tile(n)] = jnp.maximum(pre, 0.0).astype(BF)

        @pl.loop(0, D // TILE)
        def _(n):
            part[l, :, tile(n)] = dot(hid[l], wo[l, :, tile(n)]).astype(BF)

    def backward(l):
        @pl.loop(0, FS // TILE)
        def _(n):
            g = dot(whole(gb, l), wo[l, tile(n), :], 1, 1)
            gh[l, :, tile(n)] = jnp.where(
                hid[l, :, tile(n)].astype(F32) > 0.0, g, 0.0).astype(BF)

        @pl.loop(0, D // TILE)
        def _(n):
            gpart[l, :, tile(n)] = dot(gh[l], wi[l, tile(n), :], 1, 1).astype(BF)

    stores = []

    def weights(l):
        @pl.loop(0, FS // TILE)
        def _(n):
            gwo[l, tile(n), :] = dot(hid[l, :, tile(n)], whole(gb, l), 0, 0).astype(BF)

        put = pltpu.make_async_copy(gwo.at[l], gwo_o.at[l], lsem.at[2 + 2 * l])
        put.start()
        stores.append(put)

        @pl.loop(0, 2)
        def _(n):
            gwi[l, pl.ds(pl.multiple_of(n * F, F), F), :] = dot(
                xb[n, l].reshape(rows, F), gh[l], 0, 0).astype(BF)

        put = pltpu.make_async_copy(gwi.at[l], gwi_o.at[l], lsem.at[3 + 2 * l])
        put.start()
        stores.append(put)

    def half(which):
        return pl.ds(pl.multiple_of(which * F, 128), F)

    def group(p):
        top = e // (E // 2)
        return (1 - top if p == 0 else top) * (E // 2)

    def combine(own, other, stage, land, j, p):
        l = c * Lh + j
        g = group(p)
        at = pl.ds(pl.multiple_of(g * cap, cap), E // 2 * cap)
        stage[j, at, :] = (own[l, at, half(1 - h)].astype(F32)
                           + other[j, at, half(1 - h)].astype(F32)).astype(BF)
        return send(stage.at[j, at], land.at[j, at], ym)

    def finish(copy, own, other, land, final, out, j, p):
        copy.wait_recv()
        l = c * Lh + j
        g = group(p)
        at = pl.ds(pl.multiple_of(g * cap, cap), E // 2 * cap)
        total = (own[l, at, half(h)].astype(F32) + other[j, at, half(h)].astype(F32)
                 + land[j, at, :].astype(F32)).astype(BF)
        final[j, pl.ds(g, E // 2)] = total.reshape(E // 2, cap, F)
        res = []
        for k in order:
            if (k >= E // 2) == (p == 0):
                dest = flip(e, k, E)
                res.append(send(final.at[j, dest], out.at[e, j], (dest, s)))
        if p == 1:
            out[e, j] = final[j, e]
        return res

    share = -(-E // L)
    csend = []
    for j in range(Lh):
        l = (1 - c) * Lh + j
        forward(l)
        csend.append(send(part.at[l], cb.at[j], sib))
        for k in arrive[j * share:(j + 1) * share]:
            pass_on("g", gb, a2a_g, k)
    for j in range(Lh, L):
        forward(c * Lh + j - Lh)
        for k in arrive[j * share:(j + 1) * share]:
            pass_on("g", gb, a2a_g, k)
    ysend, gysend = {}, {}
    for j in range(Lh):
        csend[j].wait_recv()
        for p in range(2):
            ysend[j, p] = combine(part, cb, ys, yr, j, p)
    for k in arrive:
        pass_y("g", gb, k)
    for w in waits["g"]:
        w.wait_recv()

    steps = [(j, p) for j in range(Lh) for p in range(2)]
    gcsend, bsend, gbsend = [], [], []
    for i in range(L):
        j = i % Lh
        l = (1 - c) * Lh + j if i < Lh else c * Lh + j
        backward(l)
        if i < Lh:
            gcsend.append(send(gpart.at[l], gcb.at[j], sib))
        else:
            gcsend[j].wait_recv()
            for p in range(2):
                gysend[j, p] = combine(gpart, gcb, gys, gyr, j, p)
        for st in steps[i * 2 * Lh // L:(i + 1) * 2 * Lh // L]:
            bsend += finish(ysend[st], part, cb, yr, fin, back, *st)

    def collect(copies, out, stage, land):
        for w in copies:
            w.wait_recv()
        for n in range(T // 512):
            at = slice(n * 512, (n + 1) * 512)
            row = lax.broadcasted_iota(jnp.int32, (E * R, 512), 0)
            pick = jnp.where(row == trow[:, at], 1.0, 0.0).astype(BF)
            val = dot(out[...].reshape(E * R, F), pick, 0, 0).astype(BF)
            stage[0, :, at] = val[:Q]
            stage[1, :, at] = val[Q:]
        return send(stage.at[1 - c], land, sib)

    for i in range(L):
        weights(i)
        for st in steps[i * 2 * Lh // L:(i + 1) * 2 * Lh // L]:
            gbsend += finish(gysend[st], gpart, gcb, gyr, gfin, gback, *st)
    last = collect(bsend, back, tp, rtp)
    last.wait_recv()
    mix_o[...] = (gate[...] * (tp[c].astype(F32) + rtp[...].astype(F32))).astype(BF)
    glast = collect(gbsend, gback, gtp, rgtp)
    glast.wait_recv()
    gin_o[...] = gtp[c] + rgtp[...]
    for copy in started:
        copy.wait_send()
    for put in stores:
        put.wait()


def shards(tokens, gate, routes, grad_out, w_in, w_out):
    T, Q = tokens.shape
    E = lax.axis_size("expert")
    L, D, FS = w_in.shape
    X = E * L
    cap = 2 * T // X
    Lh = L // 2
    F = 2 * Q
    rows = E * cap
    TILE = 256
    n_sem = 2 * (6 * E + 5)
    vm = lambda shape, t=BF: pltpu.VMEM(shape, t)
    two = lambda shape: [vm(shape), vm(shape)]
    scratch = (
        [vm((1, T), jnp.int32)] + two((2, Q, T)) + two((E, Lh, cap, F)) + two((2, L, E, cap, F))
        + two((L, D, FS)) + [vm((L, D, FS)), vm((L, FS, D))]
        + two((L, rows, FS)) + two((L, rows, D)) + two((Lh, rows, D))
        + two((Lh, rows, F)) + two((Lh, rows, F)) + two((Lh, E, cap, F))
        + two((E, Lh, cap, F)) + two((2, Q, T)) + two((Q, T))
        + [pltpu.SemaphoreType.DMA((n_sem,)), pltpu.SemaphoreType.DMA((n_sem,)),
           pltpu.SemaphoreType.DMA((2 + 2 * L,))])
    V = pl.BlockSpec(memory_space=pltpu.VMEM)
    A = pl.BlockSpec(memory_space=pl.ANY)
    mix, gin, gwi, gwo = pl.pallas_call(
        functools.partial(kernel, E, cap, L, TILE),
        out_shape=(
            jax.ShapeDtypeStruct((Q, T), BF), jax.ShapeDtypeStruct((Q, T), BF),
            jax.ShapeDtypeStruct(w_in.shape, BF), jax.ShapeDtypeStruct(w_out.shape, BF)),
        in_specs=[V, V, V, V, A, A],
        out_specs=(V, V, A, A),
        scratch_shapes=scratch,
        compiler_params=pltpu.CompilerParams(
            collective_id=0, has_side_effects=True, vmem_limit_bytes=63 * 2**20),
        cost_estimate=pl.CostEstimate(
            flops=12 * L * rows * D * FS, bytes_accessed=8 * L * D * FS, transcendentals=0),
    )(routes.reshape(1, T), gate[None, :], tokens.T, grad_out.T, w_in, w_out)
    return (mix.T, gin.T, gwi, gwo)


def solution(mesh):
    in_specs = (
        P("expert", "slab"),
        P("expert"),
        P("expert", None),
        P("expert", "slab"),
        P("expert", None, "slab"),
        P("expert", "slab", None),
    )
    out_specs = (
        P("expert", "slab"),
        P("expert", "slab"),
        P("expert", None, "slab"),
        P("expert", "slab", None),
    )
    return jax.shard_map(shards, mesh=mesh, in_specs=in_specs, out_specs=out_specs, check_vma=False)
```

```python
import functools

import jax
import jax.numpy as jnp
from jax import lax
from jax.experimental import pallas as pl
from jax.experimental.pallas import tpu as pltpu
from jax.sharding import PartitionSpec as P

MESH = pl.DeviceIdType.MESH
BF = jnp.bfloat16
F32 = jnp.float32


def flip(index, mask, count):
    out = index
    bit = 1
    while bit < count:
        if mask & bit:
            out = out + (1 - 2 * ((index // bit) % 2)) * bit
        bit *= 2
    return out


def dot(a, b, ca=1, cb=0):
    return lax.dot_general(a, b, (((ca,), (cb,)), ((), ())), preferred_element_type=F32)


def kernel(E, cap, L, TILE,
           routes, gate, tok, grd, wi_h, wo_h,
           mix_o, gin_o, gwi_o, gwo_o,
           trow, cat_t, cat_g, send_t, send_g, xb, gb, wi, wo, gwi, gwo, hid, gh,
           part, gpart, cb, gcb, ys, gys, yr, gyr, fin, gfin, back, gback,
           tp, gtp, rtp, rgtp, ssem, rsem, lsem):
    Lh = L // 2
    R = Lh * cap
    Q, T = tok.shape
    F = 2 * Q
    D = 2 * F
    X = E * L
    rows = E * cap
    FS = wi.shape[2]
    e = lax.axis_index("expert")
    s = lax.axis_index("slab")
    h = s // 2
    c = s % 2
    sib = (e, 2 * h + 1 - c)
    ym = (e, 2 * (1 - h) + c)

    load_wi = pltpu.make_async_copy(wi_h, wi, lsem.at[0])
    load_wo = pltpu.make_async_copy(wo_h, wo, lsem.at[1])
    load_wi.start()
    load_wo.start()

    barrier = pltpu.get_barrier_semaphore()
    peers = [sib, ym] + [(flip(e, k, E), s) for k in range(1, E)]
    for p in peers:
        pl.semaphore_signal(barrier, inc=1, device_id=p, device_id_type=MESH)

    ids = routes[...]
    onehot = (lax.broadcasted_iota(jnp.int32, (X, T), 0) == ids).astype(F32)
    STEP = 256
    for n in range(T // STEP):
        at = slice(n * STEP, (n + 1) * STEP)
        before = (lax.broadcasted_iota(jnp.int32, (T, STEP), 0)
                  < lax.broadcasted_iota(jnp.int32, (T, STEP), 1) + n * STEP)
        earlier = dot(onehot.astype(BF), jnp.where(before, 1.0, 0.0).astype(BF))
        slot = jnp.sum(earlier * onehot[:, at], axis=0, keepdims=True).astype(jnp.int32)
        local = lax.rem(ids[:, at], L)
        trow[:, at] = jnp.where(
            lax.div(local, Lh) == c,
            lax.div(ids[:, at], L) * R + lax.rem(local, Lh) * cap + slot, -1)
    cat_g[c] = (gate[...] * grd[...].astype(F32)).astype(BF)
    cat_t[c] = tok[...]
    pl.semaphore_wait(barrier, len(peers))

    started = []

    def send(src, dst, dev):
        n = len(started)
        copy = pltpu.make_async_remote_copy(
            src_ref=src, dst_ref=dst, send_sem=ssem.at[n], recv_sem=rsem.at[n],
            device_id=dev, device_id_type=MESH)
        copy.start()
        started.append(copy)
        return copy

    far, near = list(range(E // 2, E)), list(range(1, E // 2))
    order = [k for i, f in enumerate(far) for k in ([f] + near[i:i + 1])]
    mine = pl.ds(c * Lh, Lh)

    c_t = send(cat_t.at[c], cat_t.at[c], sib)
    c_g = send(cat_g.at[c], cat_g.at[c], sib)

    def scatter(k, cat, stage, buf):
        dest = flip(e, k, E)
        row = lax.broadcasted_iota(jnp.int32, (R, T), 0) + dest * R
        place = jnp.where(row == trow[...], 1.0, 0.0).astype(BF)
        val = dot(place, cat[...].reshape(F, T), 1, 1).astype(BF).reshape(Lh, cap, F)
        if k == 0:
            buf[h, mine, e] = val
            return None
        stage[k] = val
        return send(stage.at[k], buf.at[h, mine, e], (dest, s))

    ycopy = {}
    waits = {"t": [], "g": []}

    def pass_on(tag, buf, a2a, k):
        if k:
            a2a[k].wait_recv()
        ref = buf.at[h, mine, flip(e, k, E)]
        ycopy[tag, k] = send(ref, ref, ym)
        waits[tag].append(send(ref, ref, sib))

    def pass_y(tag, buf, k):
        ycopy[tag, k].wait_recv()
        ref = buf.at[1 - h, mine, flip(e, k, E)]
        waits[tag].append(send(ref, ref, sib))

    arrive = [0] + order
    c_t.wait_recv()
    a2a_t = {k: scatter(k, cat_t, send_t, xb) for k in order + [0]}
    c_g.wait_recv()
    a2a_g = {}
    for i, k in enumerate(arrive):
        pass_on("t", xb, a2a_t, k)
        g = arrive[(i + 1) % E]
        a2a_g[g] = scatter(g, cat_g, send_g, gb)
        if i >= 2:
            pass_y("t", xb, arrive[i - 2])
    early, rest = arrive[:3], arrive[3:]
    pass_on("g", gb, a2a_g, early[0])
    for i, k in enumerate(arrive[-2:]):
        pass_y("t", xb, k)
        pass_on("g", gb, a2a_g, early[1 + i])
    for w in waits["t"]:
        w.wait_recv()
    load_wi.wait()
    load_wo.wait()

    def whole(buf, l):
        return jnp.concatenate(
            [buf[0, l].reshape(rows, F), buf[1, l].reshape(rows, F)], axis=1)

    def tile(n):
        return pl.ds(pl.multiple_of(n * TILE, TILE), TILE)

    def forward(l):
        @pl.loop(0, FS // TILE)
        def _(n):
            pre = dot(whole(xb, l), wi[l, :, tile(n)])
            hid[l, :, tile(n)] = jnp.maximum(pre, 0.0).astype(BF)

        @pl.loop(0, D // TILE)
        def _(n):
            part[l, :, tile(n)] = dot(hid[l], wo[l, :, tile(n)]).astype(BF)

    def backward(l):
        @pl.loop(0, FS // TILE)
        def _(n):
            g = dot(whole(gb, l), wo[l, tile(n), :], 1, 1)
            gh[l, :, tile(n)] = jnp.where(
                hid[l, :, tile(n)].astype(F32) > 0.0, g, 0.0).astype(BF)

        @pl.loop(0, D // TILE)
        def _(n):
            gpart[l, :, tile(n)] = dot(gh[l], wi[l, tile(n), :], 1, 1).astype(BF)

    stores = []

    def weights(l):
        @pl.loop(0, FS // TILE)
        def _(n):
            gwo[l, tile(n), :] = dot(hid[l, :, tile(n)], whole(gb, l), 0, 0).astype(BF)

        put = pltpu.make_async_copy(gwo.at[l], gwo_o.at[l], lsem.at[2 + 2 * l])
        put.start()
        stores.append(put)

        @pl.loop(0, 2)
        def _(n):
            gwi[l, pl.ds(pl.multiple_of(n * F, F), F), :] = dot(
                xb[n, l].reshape(rows, F), gh[l], 0, 0).astype(BF)

        put = pltpu.make_async_copy(gwi.at[l], gwi_o.at[l], lsem.at[3 + 2 * l])
        put.start()
        stores.append(put)

    def half(which):
        return pl.ds(pl.multiple_of(which * F, 128), F)

    def group(p):
        top = e // (E // 2)
        return (1 - top if p == 0 else top) * (E // 2)

    def combine(own, other, stage, land, j, p):
        l = c * Lh + j
        g = group(p)
        at = pl.ds(pl.multiple_of(g * cap, cap), E // 2 * cap)
        stage[j, at, :] = (own[l, at, half(1 - h)].astype(F32)
                           + other[j, at, half(1 - h)].astype(F32)).astype(BF)
        return send(stage.at[j, at], land.at[j, at], ym)

    def finish(copy, own, other, land, final, out, j, p):
        copy.wait_recv()
        l = c * Lh + j
        g = group(p)
        at = pl.ds(pl.multiple_of(g * cap, cap), E // 2 * cap)
        total = (own[l, at, half(h)].astype(F32) + other[j, at, half(h)].astype(F32)
                 + land[j, at, :].astype(F32)).astype(BF)
        final[j, pl.ds(g, E // 2)] = total.reshape(E // 2, cap, F)
        res = []
        for k in order:
            if (k >= E // 2) == (p == 0):
                dest = flip(e, k, E)
                res.append(send(final.at[j, dest], out.at[e, j], (dest, s)))
        if p == 1:
            out[e, j] = final[j, e]
        return res

    share = -(-len(rest) // L)
    csend = []
    for j in range(Lh):
        l = (1 - c) * Lh + j
        forward(l)
        csend.append(send(part.at[l], cb.at[j], sib))
        for k in rest[j * share:(j + 1) * share]:
            pass_on("g", gb, a2a_g, k)
    for j in range(Lh, L):
        forward(c * Lh + j - Lh)
        for k in rest[j * share:(j + 1) * share]:
            pass_on("g", gb, a2a_g, k)
    ysend, gysend = {}, {}
    for w in csend:
        w.wait_recv()
    steps = [(j, p) for p in range(2) for j in range(Lh)]
    for st in steps:
        ysend[st] = combine(part, cb, ys, yr, *st)
    for k in arrive:
        pass_y("g", gb, k)
    for w in waits["g"]:
        w.wait_recv()

    gcsend, bsend, gbsend = [], [], []

    def out_finish(st):
        bsend.extend(finish(ysend[st], part, cb, yr, fin, back, *st))

    def grad_finish(st):
        gbsend.extend(finish(gysend[st], gpart, gcb, gyr, gfin, gback, *st))

    for j in range(Lh):
        l = (1 - c) * Lh + j
        backward(l)
        gcsend.append(send(gpart.at[l], gcb.at[j], sib))
    out_finish(steps[0])
    for j in range(Lh):
        backward(c * Lh + j)
    for w in gcsend:
        w.wait_recv()
    for st in steps:
        gysend[st] = combine(gpart, gcb, gys, gyr, *st)
    for st in steps[1:]:
        out_finish(st)

    def collect(copies, out, stage, land):
        for w in copies:
            w.wait_recv()
        for n in range(T // 512):
            at = slice(n * 512, (n + 1) * 512)
            row = lax.broadcasted_iota(jnp.int32, (E * R, 512), 0)
            pick = jnp.where(row == trow[:, at], 1.0, 0.0).astype(BF)
            val = dot(out[...].reshape(E * R, F), pick, 0, 0).astype(BF)
            stage[0, :, at] = val[:Q]
            stage[1, :, at] = val[Q:]
        return send(stage.at[1 - c], land, sib)

    for i in range(L):
        weights(i)
        if i >= L // 2 - 1:
            grad_finish(steps[i - L // 2 + 1])
    last = collect(bsend, back, tp, rtp)
    for st in steps[L - L // 2 + 1:]:
        grad_finish(st)
    last.wait_recv()
    mix_o[...] = (gate[...] * (tp[c].astype(F32) + rtp[...].astype(F32))).astype(BF)
    glast = collect(gbsend, gback, gtp, rgtp)
    glast.wait_recv()
    gin_o[...] = gtp[c] + rgtp[...]
    for copy in started:
        copy.wait_send()
    for put in stores:
        put.wait()


def shards(tokens, gate, routes, grad_out, w_in, w_out):
    T, Q = tokens.shape
    E = lax.axis_size("expert")
    L, D, FS = w_in.shape
    X = E * L
    cap = 2 * T // X
    Lh = L // 2
    F = 2 * Q
    rows = E * cap
    TILE = 256
    n_sem = 2 * (6 * E + 5)
    vm = lambda shape, t=BF: pltpu.VMEM(shape, t)
    two = lambda shape: [vm(shape), vm(shape)]
    scratch = (
        [vm((1, T), jnp.int32)] + two((2, Q, T)) + two((E, Lh, cap, F)) + two((2, L, E, cap, F))
        + two((L, D, FS)) + [vm((L, D, FS)), vm((L, FS, D))]
        + two((L, rows, FS)) + two((L, rows, D)) + two((Lh, rows, D))
        + two((Lh, rows, F)) + two((Lh, rows, F)) + two((Lh, E, cap, F))
        + two((E, Lh, cap, F)) + two((2, Q, T)) + two((Q, T))
        + [pltpu.SemaphoreType.DMA((n_sem,)), pltpu.SemaphoreType.DMA((n_sem,)),
           pltpu.SemaphoreType.DMA((2 + 2 * L,))])
    V = pl.BlockSpec(memory_space=pltpu.VMEM)
    A = pl.BlockSpec(memory_space=pl.ANY)
    mix, gin, gwi, gwo = pl.pallas_call(
        functools.partial(kernel, E, cap, L, TILE),
        out_shape=(
            jax.ShapeDtypeStruct((Q, T), BF), jax.ShapeDtypeStruct((Q, T), BF),
            jax.ShapeDtypeStruct(w_in.shape, BF), jax.ShapeDtypeStruct(w_out.shape, BF)),
        in_specs=[V, V, V, V, A, A],
        out_specs=(V, V, A, A),
        scratch_shapes=scratch,
        compiler_params=pltpu.CompilerParams(
            collective_id=0, has_side_effects=True, vmem_limit_bytes=63 * 2**20),
        cost_estimate=pl.CostEstimate(
            flops=12 * L * rows * D * FS, bytes_accessed=8 * L * D * FS, transcendentals=0),
    )(routes.reshape(1, T), gate[None, :], tokens.T, grad_out.T, w_in, w_out)
    return (mix.T, gin.T, gwi, gwo)


def solution(mesh):
    in_specs = (
        P("expert", "slab"),
        P("expert"),
        P("expert", None),
        P("expert", "slab"),
        P("expert", None, "slab"),
        P("expert", "slab", None),
    )
    out_specs = (
        P("expert", "slab"),
        P("expert", "slab"),
        P("expert", None, "slab"),
        P("expert", "slab", None),
    )
    return jax.shard_map(shards, mesh=mesh, in_specs=in_specs, out_specs=out_specs, check_vma=False)
```
